128 devices in a mesh: section: 4 (over x), group: 32 (over y, z, core).
Axes of the slice: x: 4, y: 4, z: 4, core: 2. Of those that a mesh axis runs over, the one named last changes fastest.
Arguments:
- hidden: bfloat16 [2048, 8, 1024], P('group', None, 'section'), may hold values from -6 to 6
- pre_weight: bfloat16 [7, 1024, 512], replicated, may hold values from -0.0625 to 0.0625
- up1_weight: bfloat16 [16, 512, 256], replicated, may hold values from -0.1875 to 0.1875
- up2_weight: bfloat16 [16, 256, 128], replicated, may hold values from -0.25 to 0.25
- up3_weight: bfloat16 [4, 128, 64], replicated, may hold values from -0.375 to 0.375
- res3_weight: bfloat16 [3, 64, 64], replicated, may hold values from -0.4375 to 0.4375
- up4_weight: bfloat16 [4, 64, 32], replicated, may hold values from -0.5 to 0.5
- res4_weight: bfloat16 [3, 32, 32], replicated, may hold values from -0.625 to 0.625
- post_weight: bfloat16 [7, 32], replicated, may hold values from -0.375 to 0.375
- owner_device: int32 [2048, 1], replicated, may hold values from 0 to 31; in each aligned block of 16 rows (0 to 15, 16 to 31, ...) at most 2 rows name the same one
- stream_slot: int32 [2048], replicated, may hold values from 0 to 3
- start_frame: int32 [2048], replicated, may hold values from 0 to 56
- lead_frames: int32 [2048], replicated, may hold values from 1 to 4
- tail_frames: int32 [2048], replicated, may hold values from 1 to 4
Outputs:
- waveform: float32 [128, 4, 16384], P('group', 'section')
The draws below stay inside these ranges and needn't reach their ends.
Inputs may be any that keep to these rules, and one draw needn't show every extreme that they name: `owner_device`: in each aligned block of 16 groups (the groups of one device), no owner is named by more than 2 groups, a bound that some block reaches.
All inputs are finite; a program needn't handle non-finite values.
Results may differ from the reference program's by a relative error of at most 0.015.
Values may be sent and summed in bfloat16 or wider, within the bound.
No kernel may reach another device: no remote copies, remote signals or barrier semaphores. Data moves between devices by JAX's collectives and lax.ppermute only.
A program may use at most 128 MiB of HBM per device.

```python
import math
import jax
import jax.numpy as jnp
import numpy as np
from jax import lax

H = 1024
C0 = 512
C1 = 256
C2 = 128
C3 = 64
C4 = 32
FR = 8
OVF = 4
HOP = 256
CD = 16
STR_DEV = 4
SLF = 64
CAP = 2
GROUPS = 2048
CL = 2048
SL = 16384
SROWS = 128
SECTIONS = 4
N_GROUP = 32


def plant(entries, key, least, high):
    longest = entries.shape.index(max(entries.shape))
    spots = []
    for shift in (0, 1):
        where = [jax.random.randint(jax.random.fold_in(key, axis), (), 0, length) for axis, length in enumerate(entries.shape)]
        where[longest] = (where[longest] + shift) % entries.shape[longest]
        spots.append(tuple(where))
    return entries.at[spots[0]].set(least).at[spots[1]].set(high)


def block_levels(key, dims, cuts, low, largest):
    loudness, own = 1.0, jax.random.fold_in(key, 6)
    for axis_at, shards_of in cuts:
        draws = jnp.exp(jax.random.uniform(jax.random.fold_in(own, axis_at), (shards_of,), jnp.float32, low / len(cuts), largest / len(cuts)))
        loudness = loudness * jnp.repeat(draws, dims[axis_at] // shards_of).reshape([-1 if axis == axis_at else 1 for axis in range(len(dims))])
    return loudness


def assign_block(own_key, own, number, rows, number_of, top, limit, skew):
    order = jax.random.permutation(own_key, number_of)
    crowded, usual = load_shares(number_of, rows * top, limit, skew, True), load_shares(number_of, rows * top, limit, skew, False)
    places = jnp.arange(number_of)

    def named(sizes, rotation):
        used = int((sizes > 0).sum())
        fixed = max(1, used // 4)
        passed = fixed + (places - fixed + rotation * (used - fixed)) % max(1, number_of - fixed)
        return jnp.zeros((number_of,), jnp.int32).at[order[jnp.where(places < fixed, places, passed)]].set(jnp.asarray(sizes, jnp.int32))

    sizes = jnp.where(number % 4 == 0, named(crowded, number // 4), named(usual, number - number // 4 - 1))
    mixed = jax.random.permutation(jax.random.fold_in(own, 3), number_of)
    giver, receiver = mixed[0:number_of // 2 * 2:2], mixed[1:number_of // 2 * 2:2]
    slack = jnp.minimum(sizes[giver] - 1, limit - sizes[receiver]) // 2
    slack = jnp.where((giver == order[0]) | (receiver == order[0]) | (sizes[receiver] == 0), 0, jnp.maximum(slack, 0))
    passed = jax.random.randint(jax.random.fold_in(own, 4), (number_of // 2,), 0, 1 << 20) % (slack + 1)
    sizes = sizes.at[giver].add(-passed).at[receiver].add(passed)
    members = jnp.searchsorted(jnp.cumsum(sizes), jnp.arange(rows * top), side="right").astype(jnp.int32)
    grid = members.reshape(top, rows).T
    grid = grid[jax.random.permutation(jax.random.fold_in(own, 1), rows)]
    rotation = jax.random.randint(jax.random.fold_in(own, 2), (rows, 1), 0, top)
    return jnp.take_along_axis(grid, (jnp.arange(top)[None, :] + rotation) % top, axis=1)


def load_shares(amount, total, bound, lean, full):
    portions = [(1 << 20) // math.isqrt(rank ** lean) + 1 for rank in range(1, amount + 1)]
    largest = bound if full else min(bound, max(-(-total // amount), total * portions[0] // sum(portions)))
    least = 1 if total - largest >= amount - 1 else 0
    given, surplus = [largest] + [least] * (amount - 1), total - largest - least * (amount - 1)
    while surplus > 0:
        candidates = [i for i in range(1, amount) if given[i] < largest] or [i for i in range(1, amount) if given[i] < bound]
        whole, budget = sum([portions[i] for i in candidates]), surplus
        for i in candidates:
            extra = min(bound - given[i], max(1, budget * portions[i] // whole), surplus)
            given[i] = given[i] + extra
            surplus = surplus - extra
    return np.array(given)


def gaussian(rng, dims, spread, reach, pieces=(), kind=jnp.bfloat16):
    result = spread * jax.random.normal(rng, dims, jnp.float32)
    if pieces:
        result = result * block_levels(rng, dims, pieces, -0.22, 0.18)
    return jnp.clip(result, -reach, reach).astype(kind)


def setup_inputs(seed: int = 0) -> dict:
    seeds = jax.random.split(jax.random.key(seed), 15)
    hidden = gaussian(seeds[0], (GROUPS, FR, H), 1.0, 6.0, ((0, 32), (2, 4)))
    pre_weight = gaussian(seeds[1], (7, H, C0), (7 * H) ** -0.5, 0.0625)
    up1_weight = gaussian(seeds[2], (16, C0, C1), (2 * C0) ** -0.5, 0.1875)
    up2_weight = gaussian(seeds[3], (16, C1, C2), (2 * C1) ** -0.5, 0.25)
    up3_weight = gaussian(seeds[4], (4, C2, C3), (2 * C2) ** -0.5, 0.375)
    res3_weight = gaussian(seeds[5], (3, C3, C3), (3 * C3) ** -0.5, 0.4375)
    up4_weight = gaussian(seeds[6], (4, C3, C4), (2 * C3) ** -0.5, 0.5)
    res4_weight = gaussian(seeds[7], (3, C4, C4), (3 * C4) ** -0.5, 0.625)
    post_weight = gaussian(seeds[8], (7, C4), (7 * C4) ** -0.5, 0.375)
    owner_device_keys = jax.random.split(jax.random.fold_in(seeds[9], 1), GROUPS // CD)
    owner_device_turns = jax.random.permutation(jax.random.fold_in(seeds[9], 3), GROUPS // CD)
    owner_device = jax.vmap(lambda own, number: assign_block(jax.random.fold_in(seeds[9], 2), own, number, CD, N_GROUP, 1, CAP, 2))(owner_device_keys, owner_device_turns).reshape((GROUPS, 1))
    stream_slot = plant(jax.random.randint(seeds[10], (GROUPS,), 0, STR_DEV), jax.random.fold_in(seeds[10], 1), 0, STR_DEV - 1).astype(jnp.int32)
    start_frame = plant(jax.random.randint(seeds[11], (GROUPS,), 0, SLF - FR + 1), jax.random.fold_in(seeds[11], 1), 0, SLF - FR).astype(jnp.int32)
    lead_frames = plant(jax.random.randint(seeds[12], (GROUPS,), 1, OVF + 1), jax.random.fold_in(seeds[12], 1), 1, OVF).astype(jnp.int32)
    tail_frames = plant(jax.random.randint(seeds[13], (GROUPS,), 1, OVF + 1), jax.random.fold_in(seeds[13], 1), 1, OVF).astype(jnp.int32)
    return {"hidden": hidden, "pre_weight": pre_weight, "up1_weight": up1_weight, "up2_weight": up2_weight, "up3_weight": up3_weight, "res3_weight": res3_weight, "up4_weight": up4_weight, "res4_weight": res4_weight, "post_weight": post_weight, "owner_device": owner_device, "stream_slot": stream_slot, "start_frame": start_frame, "lead_frames": lead_frames, "tail_frames": tail_frames}


exact_mode = lax.Precision.HIGHEST


def leaky_relu(values, slope):
    return jnp.where(values >= 0, values, slope * values)


def rounded(values):
    return lax.optimization_barrier(values.astype(jnp.bfloat16))


def as_float(values):
    return values.astype(jnp.float32)


def same_conv(inputs, weight, dilation):
    tap_count = weight.shape[0]
    pad_width = (tap_count - 1) // 2 * dilation
    length = inputs.shape[2]
    padded = jnp.pad(inputs, ((0, 0), (0, 0), (pad_width, pad_width)))
    summed = jnp.zeros((inputs.shape[0], weight.shape[2], length), jnp.float32)
    for tap_id in range(tap_count):
        shifted = padded[:, :, tap_id * dilation: tap_id * dilation + length]
        summed = summed + jnp.einsum("bcl,co->bol", shifted, weight[tap_id], precision=exact_mode)
    return summed


def transposed(inputs, weight, stride):
    batch_size = inputs.shape[0]
    length = inputs.shape[2]
    tap_count = weight.shape[0]
    widened = jnp.zeros((batch_size, weight.shape[2], (length - 1) * stride + tap_count), jnp.float32)
    for tap_id in range(tap_count):
        contrib = jnp.einsum("bcl,co->bol", inputs, weight[tap_id], precision=exact_mode)
        widened = widened.at[:, :, tap_id: tap_id + (length - 1) * stride + 1: stride].add(contrib)
    offset = stride // 2
    return widened[:, :, offset: offset + length * stride]


def window(lead, tail, length):
    sample = jnp.arange(length, dtype=jnp.float32) + 0.5
    ramp_in = jnp.minimum(1.0, sample[None, :] / (HOP * as_float(lead)[:, None]))
    ramp_out = jnp.minimum(1.0, (length - sample)[None, :] / (HOP * as_float(tail)[:, None]))
    return ramp_in * ramp_out


def vocode(rows_here, weights):
    pre_w, first_w, second_w, third_w, third_res, fourth_w, fourth_res, post_w = weights
    inputs = jnp.transpose(as_float(rows_here), (0, 2, 1))
    projected = same_conv(inputs, as_float(pre_w), 1)
    active = rounded(leaky_relu(projected, 0.1))
    upsampled = transposed(as_float(active), as_float(first_w), 8)
    active = rounded(leaky_relu(upsampled, 0.1))
    upsampled = transposed(as_float(active), as_float(second_w), 8)
    active = rounded(leaky_relu(upsampled, 0.1))
    upsampled = transposed(as_float(active), as_float(third_w), 2)
    inner_act = rounded(leaky_relu(upsampled, 0.1))
    middle = upsampled + same_conv(as_float(inner_act), as_float(third_res), 3)
    active = rounded(leaky_relu(middle, 0.1))
    upsampled = transposed(as_float(active), as_float(fourth_w), 2)
    inner_act = rounded(leaky_relu(upsampled, 0.1))
    middle = upsampled + same_conv(as_float(inner_act), as_float(fourth_res), 3)
    active = rounded(leaky_relu(middle, 0.01))
    output_conv = same_conv(as_float(active), as_float(post_w)[:, :, None], 1)[:, 0]
    return jnp.tanh(output_conv)


def reference(hidden, pre_weight, up1_weight, up2_weight, up3_weight, res3_weight, up4_weight, res4_weight, post_weight, owner_device, stream_slot, start_frame, lead_frames, tail_frames):
    weights = (pre_weight, up1_weight, up2_weight, up3_weight, res3_weight, up4_weight, res4_weight, post_weight)
    blocks = GROUPS // CD

    def vocode_block(operands):
        rows_here, lead_here, tail_here = operands
        return vocode(rows_here, weights) * window(lead_here, tail_here, CL)

    waves = lax.map(vocode_block, (hidden.reshape(blocks, CD, FR, H), lead_frames.reshape(blocks, CD), tail_frames.reshape(blocks, CD)))
    waves = waves.reshape(GROUPS, CL)
    row_index = (owner_device[:, 0] * STR_DEV + stream_slot).astype(jnp.int32)
    sections = ((jnp.arange(GROUPS, dtype=jnp.int32) // CD) % SECTIONS).astype(jnp.int32)
    offsets = (start_frame * HOP).astype(jnp.int32)

    def add_group(group_id, streams):
        corner = (row_index[group_id], sections[group_id], offsets[group_id])
        current = lax.dynamic_slice(streams, corner, (1, 1, CL))
        return lax.dynamic_update_slice(streams, current + waves[group_id].reshape(1, 1, CL), corner)

    return lax.fori_loop(0, GROUPS, add_group, jnp.zeros((SROWS, SECTIONS, SL), jnp.float32))
```

```python
import jax
import jax.numpy as jnp
from jax import lax
from jax.experimental import pallas as pl
from jax.experimental.pallas import tpu as pltpu
from jax.sharding import PartitionSpec as P

CD = 16
FR = 8
SECT = 4
LANES = 32
HOP = 256
SUPER = 256
ROWS = SUPER * CD
BF = jnp.bfloat16
F32 = jnp.float32


def dot(a, b):
    return jnp.dot(a, b, preferred_element_type=F32)


def leaky(v, slope):
    return jnp.maximum(v, slope * v)


def iota(shape, dim):
    return lax.broadcasted_iota(jnp.int32, shape, dim)


def as_bf(mask):
    return jnp.where(mask, 1.0, 0.0).astype(BF)


def spread(flat, width):
    place = as_bf(iota((width, 256), 1) % width == iota((width, 256), 0))
    return dot(flat, place)


def spread_t(ref, width):
    place = as_bf(iota((width, 256), 1) % width == iota((width, 256), 0))
    return jnp.concatenate(
        [
            lax.dot_general(ref[j], place, (((0,), (0,)), ((), ())), preferred_element_type=F32)
            for j in range(ref.shape[0])
        ],
        axis=0,
    )


def blocks(rep, rows, width, entries):
    block_of = iota((rows, 256), 1) // width
    out = []
    for entry in entries:
        acc = jnp.zeros((rows, 256), F32)
        for q, j in entry:
            acc = jnp.where(block_of == q, rep[j * rows : (j + 1) * rows], acc)
        out.append(acc)
    return jnp.concatenate(out, axis=0).astype(BF)


def up_entries(places, phases):
    return [[(q, q + 1 - 2 * a) for q in range(phases) if 0 <= q + 1 - 2 * a <= 3] for a in places]


def res_entries(places, phases):
    return [
        [(q, (a - q) // 3 + 1) for q in range(phases) if a - q in (-3, 0, 3)] for a in places
    ]


def prepare(*refs):
    sources, (w2p, b3, r3, b4, r4, wc, disp, plac, win), held = refs[:11], refs[11:20], refs[20:31]
    scr, sems = refs[31:]
    copies = [pltpu.make_async_copy(a, b, sems.at[i]) for i, (a, b) in enumerate(zip(sources, held))]
    for copy in copies:
        copy.start()
    for copy in copies:
        copy.wait()
    up2, up3, res3, up4, res4, post, owners, slot, start, lead, tail = held
    section = lax.axis_index("section")
    lane = lax.axis_index("group")
    for j in range(8):
        w2p[j, :, 0:128] = up2[2 * j]
        w2p[j, :, 128:256] = up2[2 * j + 1]
    b3[...] = blocks(spread_t(up3, 64), 128, 64, up_entries((0, 1, 2, -1), 4))
    r3[...] = blocks(
        spread(res3[...].reshape(192, 64), 64), 64, 64, res_entries((*range(4), *range(-4, 0), *range(4, 8)), 4)
    )
    b4[...] = blocks(
        spread_t(up4, 32), 64, 32, up_entries((*range(4), 4, 5, -2, -1), 8)
    )
    r4[...] = blocks(
        spread(res4[...].reshape(96, 32), 32), 32, 32, res_entries((*range(8), *range(8, 12), *range(-4, 0)), 8)
    )
    scr[...] = jnp.zeros_like(scr)
    scr[0:7, 0:32] = post[...].astype(F32)
    post_t = jnp.transpose(scr[...])[0:32].astype(BF)
    tap, off = iota((128, 128), 0), iota((128, 128), 1)
    base = jnp.concatenate(
        [dot(post_t, as_bf((tap == a + 6 - off) & (tap < 7))) for a in range(8)], axis=0
    ).astype(BF)
    off, smp = iota((128, 256), 0), iota((128, 256), 1)
    for i in range(34):
        wc[i] = dot(base, as_bf((smp == 8 * (i - 1) - 3 + off) & (off < 14))).astype(BF)
    owner = jnp.concatenate([owners[:, i * 128 : (i + 1) * 128] for i in range(16)], axis=0)
    mine = jnp.where(iota((16, 128), 0) == lane // 2, 1, 0)
    spot = lane % 2 * 64 + section * CD
    rowsel = lambda v: jnp.sum(v * mine, axis=0, keepdims=True).astype(F32)
    pick = iota((128, 128), 1) == spot + iota((128, 128), 0) % CD
    column = lambda v: jnp.sum(jnp.where(pick, rowsel(v), 0.0), axis=1, keepdims=True)
    owner_col = column(owner)
    owner_row = jnp.sum(
        jnp.where(iota((128, 128), 0) == iota((128, 128), 1), owner_col, 0.0), axis=0, keepdims=True
    )
    before = (owner_col[0:CD] == owner_row) & (iota((CD, 128), 0) < iota((CD, 128), 1) % CD)
    rank = jnp.sum(jnp.where(before, 1.0, 0.0), axis=0, keepdims=True)
    dest = (2.0 * owner_row + rank).astype(jnp.int32)
    r_d, l_d = iota((512, 128), 0), iota((512, 128), 1)
    disp[...] = as_bf((r_d // FR == dest) & (r_d % FR == l_d // CD))
    t = ((iota((128, 256), 0) // CD) * HOP + iota((128, 256), 1)).astype(F32) + 0.5
    win[...] = jnp.minimum(1.0, t / (HOP * column(lead[...]))) * jnp.minimum(
        1.0, (FR * HOP - t) / (HOP * column(tail[...]))
    )
    l_g = iota((16, 128), 1)
    owned = jnp.where((l_g // CD % SECT == section) & (owner == lane), 1.0, 0.0)
    r_l, c_l = iota((128, 128), 0), iota((128, 128), 1)
    order = dot(owned.astype(BF), as_bf((r_l < c_l) & (r_l // 64 == c_l // 64)))
    target = (slot[...] * 64 + start[...]).astype(F32) * owned
    l_p = iota((16, 512), 1)
    item = jnp.zeros((16, 512), F32)
    for half in range(2):
        for c in range(2):
            at = jnp.sum(
                jnp.where((order == float(c)) & (l_g // 64 == half), target, 0.0), axis=1, keepdims=True
            )
            item = jnp.where(l_p // FR % 4 == 2 * half + c, at, item)
    item = jnp.where(l_p // 32 == iota((16, 512), 0), item, 0.0)
    goal = jnp.sum(item, axis=0, keepdims=True).astype(jnp.int32) + iota((1, 512), 1) % FR
    plac[...] = as_bf(iota((256, 512), 0) == goal)


def edges(ref, first, rows):
    return jnp.concatenate(
        [ref[pl.ds(first + 2 * CD, rows), 0:128], ref[pl.ds(first, rows), 128:256]], axis=1
    )


CHUNK = 512


def synthesize(
    hid, rec1, rec2, rec3, pre, up1_hbm, w2p, b3, r3, b4, r4, wc, disp, win, out,
    up1, xb, a0, a1, a2, u3, i3, a3, sem,
):
    section = lax.axis_index("section")
    u4, i4, a4 = u3, i3, a2
    fetch = pltpu.make_async_copy(up1_hbm, up1, sem)
    fetch.start()
    for ref, pad in ((xb, 3), (a0, 1), (a1, 1), (a2, 1), (i3, 1), (a3, 1)):
        width = ref.shape[-1]
        zero = jnp.zeros((pad * CD, width), BF)
        ref[0 : pad * CD, :] = zero
        ref[ref.shape[0] - pad * CD :, :] = zero

    r, c = iota((128, 128), 0), iota((128, 128), 1)
    turn = as_bf(c == (r % CD) * FR + r // CD)
    own = hid[pl.ds(pl.multiple_of(section * 128, 128), 128), :]
    for d, block in enumerate((own, rec1[...], rec2[...], rec3[...])):
        xb[3 * CD : 3 * CD + 128, d * 256 : (d + 1) * 256] = dot(turn, block).astype(BF)
    acc = jnp.zeros((128, 512), F32)
    for d in range(SECT):
        rows = pl.ds(pl.multiple_of(lax.rem(section + SECT - d, SECT) * 256, 256), 256)
        for j in range(7):
            acc = acc + dot(xb[j * CD : j * CD + 128, d * 256 : (d + 1) * 256], pre[j, rows, :])
    a0[CD : CD + 128, :] = leaky(acc, 0.1).astype(BF)

    fetch.wait()
    for p in range(8):
        shift, j = (0, p + 12) if p < 4 else (2 * CD, p - 4)
        y = dot(a0[CD : CD + 128, :], up1[p + 4]) + dot(a0[shift : shift + 128, :], up1[j])
        y = leaky(y, 0.1).astype(BF)
        for i in range(FR):
            at = (8 * i + p + 1) * CD
            a1[at : at + CD, :] = y[i * CD : (i + 1) * CD]

    for part in range(4):
        first = part * 256
        here = a1[first + CD : first + CD + 256, :]
        earlier = a1[first : first + 256, :]
        later = a1[first + 2 * CD : first + 2 * CD + 256, :]
        for q in range(4):
            side, j = (earlier, q + 6) if q < 2 else (later, q - 2)
            y = leaky(dot(here, w2p[q + 2]) + dot(side, w2p[j]), 0.1).astype(BF)
            for i in range(16):
                at = (4 * (part * 16 + i) + q + 1) * CD
                a2[at : at + CD, :] = y[i * CD : (i + 1) * CD]

    def each(body):
        @pl.loop(0, ROWS // CHUNK)
        def _(n):
            body(pl.multiple_of(n * CHUNK, CHUNK))

    @each
    def _(first):
        y = dot(a2[pl.ds(first + CD, CHUNK), :], b3[0:256, :])
        y = y + dot(edges(a2, first, CHUNK), b3[256:512, :])
        u3[pl.ds(first, CHUNK), :] = y
        i3[pl.ds(first + CD, CHUNK), :] = leaky(y, 0.1).astype(BF)

    @each
    def _(first):
        y = u3[pl.ds(first, CHUNK), :] + dot(i3[pl.ds(first + CD, CHUNK), :], r3[0:256, :])
        y = y + dot(i3[pl.ds(first, CHUNK), :], r3[256:512, :])
        y = y + dot(i3[pl.ds(first + 2 * CD, CHUNK), :], r3[512:768, :])
        a3[pl.ds(first + CD, CHUNK), :] = leaky(y, 0.1).astype(BF)

    @each
    def _(first):
        y = dot(a3[pl.ds(first + CD, CHUNK), :], b4[0:256, :])
        y = y + dot(edges(a3, first, CHUNK), b4[256:512, :])
        u4[pl.ds(first, CHUNK), :] = y
        i4[pl.ds(first + CD, CHUNK), :] = leaky(y, 0.1).astype(BF)

    @each
    def _(first):
        y = u4[pl.ds(first, CHUNK), :] + dot(i4[pl.ds(first + CD, CHUNK), :], r4[0:256, :])
        y = y + dot(edges(i4, first, CHUNK), r4[256:512, :])
        a4[pl.ds(first + CD, CHUNK), :] = leaky(y, 0.01).astype(BF)

    acc = jnp.zeros((128, 256), F32)
    for i in range(34):
        rows = [a4[fr * 512 + i * CD : fr * 512 + (i + 1) * CD, :] for fr in range(FR)]
        acc = acc + dot(jnp.concatenate(rows, axis=0), wc[i])
    wave = (jnp.tanh(acc) * win[...]).astype(BF)
    out[...] = dot(disp[...], wave).astype(BF)


def place(plac, rec, out):
    y = dot(plac[...], rec[...])
    out[pl.ds(0, 256, stride=2), :] = y[:, 0:128]
    out[pl.ds(1, 256, stride=2), :] = y[:, 128:256]


VM = pl.BlockSpec(memory_space=pltpu.VMEM)
HB = pl.BlockSpec(memory_space=pltpu.HBM)
LIMIT = 24 * 1024 * 1024


def shards(
    hidden, pre_weight, up1_weight, up2_weight, up3_weight, res3_weight, up4_weight, res4_weight,
    post_weight, owner_device, stream_slot, start_frame, lead_frames, tail_frames,
):
    section = lax.axis_index("section")
    rows_here = hidden.reshape(SECT, 128, 256)
    received = []
    for d in (1, 2, 3):
        block = lax.dynamic_index_in_dim(rows_here, (section + d) % SECT, 0, keepdims=False)
        received.append(lax.ppermute(block, "section", [(i, (i + d) % SECT) for i in range(SECT)]))
    shape = jax.ShapeDtypeStruct
    prepared = pl.pallas_call(
        prepare,
        out_shape=(
            shape((8, 256, 256), BF),
            shape((512, 256), BF),
            shape((768, 256), BF),
            shape((512, 256), BF),
            shape((512, 256), BF),
            shape((34, 256, 256), BF),
            shape((512, 128), BF),
            shape((256, 512), BF),
            shape((128, 256), F32),
        ),
        in_specs=[HB] * 11,
        out_specs=(VM,) * 9,
        scratch_shapes=[
            pltpu.VMEM((16, 256, 128), BF),
            pltpu.VMEM((4, 64, 128), BF),
            pltpu.VMEM((3, 64, 64), BF),
            pltpu.VMEM((4, 32, 64), BF),
            pltpu.VMEM((3, 32, 32), BF),
            pltpu.VMEM((7, 32), BF),
            pltpu.VMEM((1, 2048), jnp.int32),
            *[pltpu.VMEM((16, 128), jnp.int32)] * 4,
            pltpu.VMEM((128, 128), F32),
            pltpu.SemaphoreType.DMA((11,)),
        ],
        compiler_params=pltpu.CompilerParams(vmem_limit_bytes=16 * 1024 * 1024),
        cost_estimate=pl.CostEstimate(flops=2_000_000_000, bytes_accessed=8_000_000, transcendentals=0),
        name="prepare",
    )(
        *(
            pltpu.with_memory_space_constraint(v, pltpu.HBM)
            for v in (
                up2_weight, jnp.swapaxes(up3_weight, 1, 2), res3_weight, jnp.swapaxes(up4_weight, 1, 2),
                res4_weight, post_weight, owner_device.reshape(1, 2048),
                *(v.reshape(16, 128) for v in (stream_slot, start_frame, lead_frames, tail_frames)),
            )
        )
    )
    w2p, b3, r3, b4, r4, wc, disp, plac, win = prepared
    sent = pl.pallas_call(
        synthesize,
        out_shape=shape((512, 256), BF),
        in_specs=[VM] * 5 + [HB] + [VM] * 8,
        out_specs=VM,
        scratch_shapes=[
            pltpu.VMEM((16, 512, 256), BF),
            pltpu.VMEM((128 + 6 * CD, 1024), BF),
            pltpu.VMEM((128 + 2 * CD, 512), BF),
            pltpu.VMEM((1024 + 2 * CD, 256), BF),
            pltpu.VMEM((ROWS + 2 * CD, 256), BF),
            pltpu.VMEM((ROWS, 256), F32),
            pltpu.VMEM((ROWS + 2 * CD, 256), BF),
            pltpu.VMEM((ROWS + 2 * CD, 256), BF),
            pltpu.SemaphoreType.DMA,
        ],
        compiler_params=pltpu.CompilerParams(vmem_limit_bytes=LIMIT),
        cost_estimate=pl.CostEstimate(
            flops=8_000_000_000, bytes_accessed=20_000_000, transcendentals=32768
        ),
        name="synthesize",
    )(hidden.reshape(512, 256), *received, pre_weight, pltpu.with_memory_space_constraint(up1_weight, pltpu.HBM), w2p, b3, r3, b4, r4, wc, disp, win)
    waves = lax.all_to_all(sent, "group", split_axis=0, concat_axis=0, tiled=True)
    streams = pl.pallas_call(
        place,
        out_shape=shape((512, 128), F32),
        in_specs=[VM] * 2,
        out_specs=VM,
        compiler_params=pltpu.CompilerParams(vmem_limit_bytes=8 * 1024 * 1024),
        name="place",
    )(plac, waves)
    return streams.reshape(4, 1, 64 * HOP)


def solution(mesh):
    in_specs = (P("group", None, "section"),) + (P(),) * 13
    return jax.shard_map(
        shards, mesh=mesh, in_specs=in_specs, out_specs=P("group", "section", None), check_vma=False
    )
```

```python
import jax
import jax.numpy as jnp
from jax import lax
from jax.experimental import pallas as pl
from jax.experimental.pallas import tpu as pltpu
from jax.sharding import PartitionSpec as P

CD = 16
FR = 8
SECT = 4
LANES = 32
HOP = 256
SUPER = 256
ROWS = SUPER * CD
BF = jnp.bfloat16
F32 = jnp.float32


def dot(a, b):
    return jnp.dot(a, b, preferred_element_type=F32)


def leaky(v, slope):
    return jnp.maximum(v, slope * v)


def iota(shape, dim):
    return lax.broadcasted_iota(jnp.int32, shape, dim)


def as_bf(mask):
    return jnp.where(mask, 1.0, 0.0).astype(BF)


def spread(flat, width):
    place = as_bf(iota((width, 256), 1) % width == iota((width, 256), 0))
    return dot(flat, place)


def spread_t(ref, width):
    place = as_bf(iota((width, 256), 1) % width == iota((width, 256), 0))
    return jnp.concatenate(
        [
            lax.dot_general(ref[j], place, (((0,), (0,)), ((), ())), preferred_element_type=F32)
            for j in range(ref.shape[0])
        ],
        axis=0,
    )


def blocks(rep, rows, width, entries):
    block_of = iota((rows, 256), 1) // width
    out = []
    for entry in entries:
        acc = jnp.zeros((rows, 256), F32)
        for q, j in entry:
            acc = jnp.where(block_of == q, rep[j * rows : (j + 1) * rows], acc)
        out.append(acc)
    return jnp.concatenate(out, axis=0).astype(BF)


def up_entries(places, phases):
    return [[(q, q + 1 - 2 * a) for q in range(phases) if 0 <= q + 1 - 2 * a <= 3] for a in places]


def res_entries(places, phases):
    return [
        [(q, (a - q) // 3 + 1) for q in range(phases) if a - q in (-3, 0, 3)] for a in places
    ]


def prepare(*refs):
    sources, (up1, w2p, b3, r3, b4, r4, wc, disp, plac, win), held = refs[:12], refs[12:22], refs[22:33]
    scr, sems = refs[33:]
    copies = [pltpu.make_async_copy(a, b, sems.at[i]) for i, (a, b) in enumerate(zip(sources, (*held, up1)))]
    for copy in copies:
        copy.start()
    for copy in copies[:11]:
        copy.wait()
    up2, up3, res3, up4, res4, post, owners, slot, start, lead, tail = held
    section = lax.axis_index("section")
    lane = lax.axis_index("group")
    for j in range(8):
        w2p[j, :, 0:128] = up2[2 * j]
        w2p[j, :, 128:256] = up2[2 * j + 1]
    b3[...] = blocks(spread_t(up3, 64), 128, 64, up_entries((0, 1, 2, -1), 4))
    r3[...] = blocks(
        spread(res3[...].reshape(192, 64), 64), 64, 64, res_entries((*range(4), *range(-4, 0), *range(4, 8)), 4)
    )
    b4[...] = blocks(
        spread_t(up4, 32), 64, 32, up_entries((*range(4), 4, 5, -2, -1), 8)
    )
    r4[...] = blocks(
        spread(res4[...].reshape(96, 32), 32), 32, 32, res_entries((*range(8), *range(8, 12), *range(-4, 0)), 8)
    )
    scr[...] = jnp.zeros_like(scr)
    scr[0:7, 0:32] = post[...].astype(F32)
    post_t = jnp.transpose(scr[...])[0:32].astype(BF)
    tap, off = iota((128, 128), 0), iota((128, 128), 1)
    base = jnp.concatenate(
        [dot(post_t, as_bf((tap == a + 6 - off) & (tap < 7))) for a in range(8)], axis=0
    ).astype(BF)
    off, smp = iota((128, 256), 0), iota((128, 256), 1)
    for i in range(34):
        wc[i] = dot(base, as_bf((smp == 8 * (i - 1) - 3 + off) & (off < 14))).astype(BF)
    owner = jnp.concatenate([owners[:, i * 128 : (i + 1) * 128] for i in range(16)], axis=0)
    mine = jnp.where(iota((16, 128), 0) == lane // 2, 1, 0)
    spot = lane % 2 * 64 + section * CD
    rowsel = lambda v: jnp.sum(v * mine, axis=0, keepdims=True).astype(F32)
    pick = iota((128, 128), 1) == spot + iota((128, 128), 0) % CD
    column = lambda v: jnp.sum(jnp.where(pick, rowsel(v), 0.0), axis=1, keepdims=True)
    owner_col = column(owner)
    owner_row = jnp.sum(
        jnp.where(iota((128, 128), 0) == iota((128, 128), 1), owner_col, 0.0), axis=0, keepdims=True
    )
    before = (owner_col[0:CD] == owner_row) & (iota((CD, 128), 0) < iota((CD, 128), 1) % CD)
    rank = jnp.sum(jnp.where(before, 1.0, 0.0), axis=0, keepdims=True)
    dest = (2.0 * owner_row + rank).astype(jnp.int32)
    r_d, l_d = iota((512, 128), 0), iota((512, 128), 1)
    disp[...] = as_bf((r_d // FR == dest) & (r_d % FR == l_d // CD))
    t = ((iota((128, 256), 0) // CD) * HOP + iota((128, 256), 1)).astype(F32) + 0.5
    win[...] = jnp.minimum(1.0, t / (HOP * column(lead[...]))) * jnp.minimum(
        1.0, (FR * HOP - t) / (HOP * column(tail[...]))
    )
    l_g = iota((16, 128), 1)
    owned = jnp.where((l_g // CD % SECT == section) & (owner == lane), 1.0, 0.0)
    r_l, c_l = iota((128, 128), 0), iota((128, 128), 1)
    order = dot(owned.astype(BF), as_bf((r_l < c_l) & (r_l // 64 == c_l // 64)))
    target = (slot[...] * 64 + start[...]).astype(F32) * owned
    l_p = iota((16, 512), 1)
    item = jnp.zeros((16, 512), F32)
    for half in range(2):
        for c in range(2):
            at = jnp.sum(
                jnp.where((order == float(c)) & (l_g // 64 == half), target, 0.0), axis=1, keepdims=True
            )
            item = jnp.where(l_p // FR % 4 == 2 * half + c, at, item)
    item = jnp.where(l_p // 32 == iota((16, 512), 0), item, 0.0)
    goal = jnp.sum(item, axis=0, keepdims=True).astype(jnp.int32) + iota((1, 512), 1) % FR
    plac[...] = as_bf(iota((256, 512), 0) == goal)
    copies[11].wait()


def edges(ref, first, rows):
    return jnp.concatenate(
        [ref[first + 2 * CD : first + 2 * CD + rows, 0:128], ref[first : first + rows, 128:256]], axis=1
    )


CHUNK = 512


def synthesize(
    hid, rec1, rec2, rec3, pre, up1, w2p, b3, r3, b4, r4, wc, disp, win, out,
    xb, a0, a1, a2, u3, i3, a3, u4, i4, a4,
):
    section = lax.axis_index("section")
    for ref, pad in ((xb, 3), (a0, 1), (a1, 1), (a2, 1), (i3, 1), (a3, 1), (i4, 1), (a4, 1)):
        width = ref.shape[-1]
        zero = jnp.zeros((pad * CD, width), BF)
        ref[0 : pad * CD, :] = zero
        ref[ref.shape[0] - pad * CD :, :] = zero

    r, c = iota((128, 128), 0), iota((128, 128), 1)
    turn = as_bf(c == (r % CD) * FR + r // CD)
    own = hid[pl.ds(pl.multiple_of(section * 128, 128), 128), :]
    for d, block in enumerate((own, rec1[...], rec2[...], rec3[...])):
        xb[3 * CD : 3 * CD + 128, d * 256 : (d + 1) * 256] = dot(turn, block).astype(BF)
    acc = jnp.zeros((128, 512), F32)
    for d in range(SECT):
        rows = pl.ds(pl.multiple_of(lax.rem(section + SECT - d, SECT) * 256, 256), 256)
        for j in range(7):
            acc = acc + dot(xb[j * CD : j * CD + 128, d * 256 : (d + 1) * 256], pre[j, rows, :])
    a0[CD : CD + 128, :] = leaky(acc, 0.1).astype(BF)

    for p in range(8):
        shift, j = (0, p + 12) if p < 4 else (2 * CD, p - 4)
        y = dot(a0[CD : CD + 128, :], up1[p + 4]) + dot(a0[shift : shift + 128, :], up1[j])
        y = leaky(y, 0.1).astype(BF)
        for i in range(FR):
            at = (8 * i + p + 1) * CD
            a1[at : at + CD, :] = y[i * CD : (i + 1) * CD]

    for part in range(4):
        first = part * 256
        here = a1[first + CD : first + CD + 256, :]
        earlier = a1[first : first + 256, :]
        later = a1[first + 2 * CD : first + 2 * CD + 256, :]
        for q in range(4):
            side, j = (earlier, q + 6) if q < 2 else (later, q - 2)
            y = leaky(dot(here, w2p[q + 2]) + dot(side, w2p[j]), 0.1).astype(BF)
            for i in range(16):
                at = (4 * (part * 16 + i) + q + 1) * CD
                a2[at : at + CD, :] = y[i * CD : (i + 1) * CD]

    def third(lo, hi):
        rows = hi - lo
        y = dot(jnp.concatenate([a2[lo + CD : hi + CD, :], edges(a2, lo, rows)], axis=1), b3[...])
        u3[lo:hi, :] = y
        i3[lo + CD : hi + CD, :] = leaky(y, 0.1).astype(BF)

    def third_res(lo, hi):
        near = [i3[lo + CD : hi + CD, :], i3[lo:hi, :], i3[lo + 2 * CD : hi + 2 * CD, :]]
        y = u3[lo:hi, :] + dot(jnp.concatenate(near, axis=1), r3[...])
        a3[lo + CD : hi + CD, :] = leaky(y, 0.1).astype(BF)

    def fourth(lo, hi):
        rows = hi - lo
        y = dot(jnp.concatenate([a3[lo + CD : hi + CD, :], edges(a3, lo, rows)], axis=1), b4[...])
        u4[lo:hi, :] = y
        i4[lo + CD : hi + CD, :] = leaky(y, 0.1).astype(BF)

    def fourth_res(lo, hi):
        rows = hi - lo
        y = u4[lo:hi, :] + dot(
            jnp.concatenate([i4[lo + CD : hi + CD, :], edges(i4, lo, rows)], axis=1), r4[...]
        )
        a4[lo + CD : hi + CD, :] = leaky(y, 0.01).astype(BF)

    stages = (third, third_res, fourth, fourth_res)
    chunks = ROWS // CHUNK
    for step in range(chunks + len(stages) - 1):
        for behind in reversed(range(len(stages))):
            n = step - behind
            if 0 <= n < chunks:
                lo = max(0, n * CHUNK - behind * CD)
                hi = ROWS if n == chunks - 1 else (n + 1) * CHUNK - behind * CD
                stages[behind](lo, hi)

    acc = jnp.zeros((128, 256), F32)
    for i in range(34):
        rows = [a4[fr * 512 + i * CD : fr * 512 + (i + 1) * CD, :] for fr in range(FR)]
        acc = acc + dot(jnp.concatenate(rows, axis=0), wc[i])
    wave = (jnp.tanh(acc) * win[...]).astype(BF)
    out[...] = dot(disp[...], wave).astype(BF)


def place(plac, rec, out):
    y = dot(plac[...], rec[...])
    out[pl.ds(0, 256, stride=2), :] = y[:, 0:128]
    out[pl.ds(1, 256, stride=2), :] = y[:, 128:256]


VM = pl.BlockSpec(memory_space=pltpu.VMEM)
HB = pl.BlockSpec(memory_space=pltpu.HBM)
LIMIT = 33 * 1024 * 1024


def shards(
    hidden, pre_weight, up1_weight, up2_weight, up3_weight, res3_weight, up4_weight, res4_weight,
    post_weight, owner_device, stream_slot, start_frame, lead_frames, tail_frames,
):
    section = lax.axis_index("section")
    rows_here = hidden.reshape(SECT, 128, 256)
    received = []
    for d in (1, 2, 3):
        block = lax.dynamic_index_in_dim(rows_here, (section + d) % SECT, 0, keepdims=False)
        received.append(lax.ppermute(block, "section", [(i, (i + d) % SECT) for i in range(SECT)]))
    shape = jax.ShapeDtypeStruct
    prepared = pl.pallas_call(
        prepare,
        out_shape=(
            shape((16, 512, 256), BF),
            shape((8, 256, 256), BF),
            shape((512, 256), BF),
            shape((768, 256), BF),
            shape((512, 256), BF),
            shape((512, 256), BF),
            shape((34, 256, 256), BF),
            shape((512, 128), BF),
            shape((256, 512), BF),
            shape((128, 256), F32),
        ),
        in_specs=[HB] * 12,
        out_specs=(VM,) * 10,
        scratch_shapes=[
            pltpu.VMEM((16, 256, 128), BF),
            pltpu.VMEM((4, 64, 128), BF),
            pltpu.VMEM((3, 64, 64), BF),
            pltpu.VMEM((4, 32, 64), BF),
            pltpu.VMEM((3, 32, 32), BF),
            pltpu.VMEM((7, 32), BF),
            pltpu.VMEM((1, 2048), jnp.int32),
            *[pltpu.VMEM((16, 128), jnp.int32)] * 4,
            pltpu.VMEM((128, 128), F32),
            pltpu.SemaphoreType.DMA((12,)),
        ],
        compiler_params=pltpu.CompilerParams(vmem_limit_bytes=14 * 1024 * 1024),
        cost_estimate=pl.CostEstimate(flops=2_000_000_000, bytes_accessed=8_000_000, transcendentals=0),
        name="prepare",
    )(
        *(
            pltpu.with_memory_space_constraint(v, pltpu.HBM)
            for v in (
                up2_weight, jnp.swapaxes(up3_weight, 1, 2), res3_weight, jnp.swapaxes(up4_weight, 1, 2),
                res4_weight, post_weight, owner_device.reshape(1, 2048),
                *(v.reshape(16, 128) for v in (stream_slot, start_frame, lead_frames, tail_frames)),
                up1_weight,
            )
        )
    )
    up1, w2p, b3, r3, b4, r4, wc, disp, plac, win = prepared
    sent = pl.pallas_call(
        synthesize,
        out_shape=shape((512, 256), BF),
        in_specs=[VM] * 14,
        out_specs=VM,
        scratch_shapes=[
            pltpu.VMEM((128 + 6 * CD, 1024), BF),
            pltpu.VMEM((128 + 2 * CD, 512), BF),
            pltpu.VMEM((1024 + 2 * CD, 256), BF),
            pltpu.VMEM((ROWS + 2 * CD, 256), BF),
            pltpu.VMEM((ROWS, 256), F32),
            pltpu.VMEM((ROWS + 2 * CD, 256), BF),
            pltpu.VMEM((ROWS + 2 * CD, 256), BF),
            pltpu.VMEM((ROWS, 256), F32),
            pltpu.VMEM((ROWS + 2 * CD, 256), BF),
            pltpu.VMEM((ROWS + 2 * CD, 256), BF),
        ],
        compiler_params=pltpu.CompilerParams(vmem_limit_bytes=LIMIT),
        cost_estimate=pl.CostEstimate(
            flops=8_000_000_000, bytes_accessed=20_000_000, transcendentals=32768
        ),
        name="synthesize",
    )(hidden.reshape(512, 256), *received, pre_weight, up1, w2p, b3, r3, b4, r4, wc, disp, win)
    waves = lax.all_to_all(sent, "group", split_axis=0, concat_axis=0, tiled=True)
    streams = pl.pallas_call(
        place,
        out_shape=shape((512, 128), F32),
        in_specs=[VM] * 2,
        out_specs=VM,
        compiler_params=pltpu.CompilerParams(vmem_limit_bytes=8 * 1024 * 1024),
        name="place",
    )(plac, waves)
    return streams.reshape(4, 1, 64 * HOP)


def solution(mesh):
    in_specs = (P("group", None, "section"),) + (P(),) * 13
    return jax.shard_map(
        shards, mesh=mesh, in_specs=in_specs, out_specs=P("group", "section", None), check_vma=False
    )
```

```python
import jax
import jax.numpy as jnp
from jax import lax
from jax.experimental import pallas as pl
from jax.experimental.pallas import tpu as pltpu
from jax.sharding import PartitionSpec as P

CD = 16
FR = 8
SECT = 4
LANES = 32
HOP = 256
SUPER = 256
ROWS = SUPER * CD
BF = jnp.bfloat16
F32 = jnp.float32


def dot(a, b):
    return jnp.dot(a, b, preferred_element_type=F32)


def leaky(v, slope):
    return jnp.maximum(v, slope * v)


def iota(shape, dim):
    return lax.broadcasted_iota(jnp.int32, shape, dim)


def as_bf(mask):
    return jnp.where(mask, 1.0, 0.0).astype(BF)


def spread(flat, width):
    place = as_bf(iota((width, 256), 1) % width == iota((width, 256), 0))
    return dot(flat, place)


def spread_t(ref, width):
    place = as_bf(iota((width, 256), 1) % width == iota((width, 256), 0))
    return jnp.concatenate(
        [
            lax.dot_general(ref[j], place, (((0,), (0,)), ((), ())), preferred_element_type=F32)
            for j in range(ref.shape[0])
        ],
        axis=0,
    )


def blocks(rep, rows, width, entries):
    block_of = iota((rows, 256), 1) // width
    out = []
    for entry in entries:
        acc = jnp.zeros((rows, 256), F32)
        for q, j in entry:
            acc = jnp.where(block_of == q, rep[j * rows : (j + 1) * rows], acc)
        out.append(acc)
    return jnp.concatenate(out, axis=0).astype(BF)


def up_entries(places, phases):
    return [[(q, q + 1 - 2 * a) for q in range(phases) if 0 <= q + 1 - 2 * a <= 3] for a in places]


def res_entries(places, phases):
    return [
        [(q, (a - q) // 3 + 1) for q in range(phases) if a - q in (-3, 0, 3)] for a in places
    ]


def prepare(*refs):
    sources, (up1, w2p, b3, r3, b4, r4, wc, disp, plac, win), held = refs[:12], refs[12:22], refs[22:33]
    scr, sems = refs[33:]
    copies = [pltpu.make_async_copy(a, b, sems.at[i]) for i, (a, b) in enumerate(zip(sources, (*held, up1)))]
    for copy in copies:
        copy.start()
    post, up3, res3, up4, res4, owners, slot, start, lead, tail, up2 = held
    section = lax.axis_index("section")
    lane = lax.axis_index("group")
    for copy in copies[:10]:
        copy.wait()
    b3[...] = blocks(spread_t(up3, 64), 128, 64, up_entries((0, 1, 2, -1), 4))
    r3[...] = blocks(
        spread(res3[...].reshape(192, 64), 64), 64, 64, res_entries((*range(4), *range(-4, 0), *range(4, 8)), 4)
    )
    b4[...] = blocks(
        spread_t(up4, 32), 64, 32, up_entries((*range(4), 4, 5, -2, -1), 8)
    )
    r4[...] = blocks(
        spread(res4[...].reshape(96, 32), 32), 32, 32, res_entries((*range(8), *range(8, 12), *range(-4, 0)), 8)
    )
    scr[...] = jnp.zeros_like(scr)
    scr[0:7, 0:32] = post[...].astype(F32)
    post_t = jnp.transpose(scr[...])[0:32].astype(BF)
    tap, off = iota((128, 128), 0), iota((128, 128), 1)
    base = jnp.concatenate(
        [dot(post_t, as_bf((tap == a + 6 - off) & (tap < 7))) for a in range(8)], axis=0
    ).astype(BF)
    off, smp = iota((128, 256), 0), iota((128, 256), 1)
    for i in range(9):
        first = jnp.where(smp < 128, 8 * (i - 1) - 3, 128 + 8 * (i + 8) - 3)
        both = dot(base, as_bf((smp == first + off) & (off < 14)))
        wc[i] = both[:, 0:128].astype(BF)
        wc[i + 9] = both[:, 128:256].astype(BF)
    owner = jnp.concatenate([owners[:, i * 128 : (i + 1) * 128] for i in range(16)], axis=0)
    mine = jnp.where(iota((16, 128), 0) == lane // 2, 1, 0)
    spot = lane % 2 * 64 + section * CD
    rowsel = lambda v: jnp.sum(v * mine, axis=0, keepdims=True).astype(F32)
    pick = iota((256, 128), 1) == spot + iota((256, 128), 0) % CD
    column = lambda v: jnp.sum(jnp.where(pick, rowsel(v), 0.0), axis=1, keepdims=True)
    owner_col = column(owner)[0:128]
    owner_row = jnp.sum(
        jnp.where(iota((128, 128), 0) == iota((128, 128), 1), owner_col, 0.0), axis=0, keepdims=True
    )
    before = (owner_col[0:CD] == owner_row) & (iota((CD, 128), 0) < iota((CD, 128), 1) % CD)
    rank = jnp.sum(jnp.where(before, 1.0, 0.0), axis=0, keepdims=True)
    dest = (2.0 * owner_row + rank).astype(jnp.int32)
    r_d, l_d = iota((512, 128), 0), iota((512, 128), 1)
    disp[...] = as_bf((r_d // FR == dest) & (r_d % FR == l_d // CD))
    t = ((iota((256, 128), 0) // CD) * 128 + iota((256, 128), 1)).astype(F32) + 0.5
    win[...] = jnp.minimum(1.0, t / (HOP * column(lead[...]))) * jnp.minimum(
        1.0, (FR * HOP - t) / (HOP * column(tail[...]))
    )
    l_g = iota((16, 128), 1)
    owned = jnp.where((l_g // CD % SECT == section) & (owner == lane), 1.0, 0.0)
    r_l, c_l = iota((128, 128), 0), iota((128, 128), 1)
    order = dot(owned.astype(BF), as_bf((r_l < c_l) & (r_l // 64 == c_l // 64)))
    target = (slot[...] * 64 + start[...]).astype(F32) * owned
    l_p = iota((16, 512), 1)
    item = jnp.zeros((16, 512), F32)
    for half in range(2):
        for c in range(2):
            at = jnp.sum(
                jnp.where((order == float(c)) & (l_g // 64 == half), target, 0.0), axis=1, keepdims=True
            )
            item = jnp.where(l_p // FR % 4 == 2 * half + c, at, item)
    item = jnp.where(l_p // 32 == iota((16, 512), 0), item, 0.0)
    goal = jnp.sum(item, axis=0, keepdims=True).astype(jnp.int32) + iota((1, 512), 1) % FR
    plac[...] = as_bf(iota((256, 512), 0) == goal)
    copies[10].wait()
    for j in range(8):
        w2p[j, :, 0:128] = up2[2 * j]
        w2p[j, :, 128:256] = up2[2 * j + 1]
    copies[11].wait()


def edges(ref, first, rows):
    return jnp.concatenate(
        [ref[first + 2 * CD : first + 2 * CD + rows, 0:128], ref[first : first + rows, 128:256]], axis=1
    )


CHUNK = 512


def synthesize(
    own, rec1, rec2, rec3, pre, up1, w2p, b3, r3, b4, r4, wc, disp, win, out,
    xb, a0, a1, a2, u3, i3, a3, u4, i4, a4,
):
    section = lax.axis_index("section")
    for ref, pad in ((xb, 3), (a0, 1), (a1, 1), (a2, 1), (i3, 1), (a3, 1), (i4, 1), (a4, 1)):
        width = ref.shape[-1]
        zero = jnp.zeros((pad * CD, width), BF)
        ref[0 : pad * CD, :] = zero
        ref[ref.shape[0] - pad * CD :, :] = zero

    r, c = iota((128, 128), 0), iota((128, 128), 1)
    turn = as_bf(c == (r % CD) * FR + r // CD)
    for d, block in enumerate((own[...], rec1[...], rec2[...], rec3[...])):
        xb[3 * CD : 3 * CD + 128, d * 256 : (d + 1) * 256] = dot(turn, block).astype(BF)
    acc = jnp.zeros((128, 512), F32)
    for d in range(SECT):
        rows = pl.ds(pl.multiple_of(lax.rem(section + SECT - d, SECT) * 256, 256), 256)
        for j in range(7):
            acc = acc + dot(xb[j * CD : j * CD + 128, d * 256 : (d + 1) * 256], pre[j, rows, :])
    a0[CD : CD + 128, :] = leaky(acc, 0.1).astype(BF)

    for p in range(8):
        shift, j = (0, p + 12) if p < 4 else (2 * CD, p - 4)
        y = dot(a0[CD : CD + 128, :], up1[p + 4]) + dot(a0[shift : shift + 128, :], up1[j])
        y = leaky(y, 0.1).astype(BF)
        for i in range(FR):
            at = (8 * i + p + 1) * CD
            a1[at : at + CD, :] = y[i * CD : (i + 1) * CD]

    for part in range(4):
        first = part * 256
        here = a1[first + CD : first + CD + 256, :]
        earlier = a1[first : first + 256, :]
        later = a1[first + 2 * CD : first + 2 * CD + 256, :]
        for q in range(4):
            side, j = (earlier, q + 6) if q < 2 else (later, q - 2)
            y = leaky(dot(here, w2p[q + 2]) + dot(side, w2p[j]), 0.1).astype(BF)
            for i in range(16):
                at = (4 * (part * 16 + i) + q + 1) * CD
                a2[at : at + CD, :] = y[i * CD : (i + 1) * CD]

    def third(lo, hi):
        rows = hi - lo
        y = dot(jnp.concatenate([a2[lo + CD : hi + CD, :], edges(a2, lo, rows)], axis=1), b3[...])
        u3[lo:hi, :] = y
        i3[lo + CD : hi + CD, :] = leaky(y, 0.1).astype(BF)

    def third_res(lo, hi):
        near = [i3[lo + CD : hi + CD, :], i3[lo:hi, :], i3[lo + 2 * CD : hi + 2 * CD, :]]
        y = u3[lo:hi, :] + dot(jnp.concatenate(near, axis=1), r3[...])
        a3[lo + CD : hi + CD, :] = leaky(y, 0.1).astype(BF)

    def fourth(lo, hi):
        rows = hi - lo
        y = dot(jnp.concatenate([a3[lo + CD : hi + CD, :], edges(a3, lo, rows)], axis=1), b4[...])
        u4[lo:hi, :] = y
        i4[lo + CD : hi + CD, :] = leaky(y, 0.1).astype(BF)

    def fourth_res(lo, hi):
        rows = hi - lo
        y = u4[lo:hi, :] + dot(
            jnp.concatenate([i4[lo + CD : hi + CD, :], edges(i4, lo, rows)], axis=1), r4[...]
        )
        a4[lo + CD : hi + CD, :] = leaky(y, 0.01).astype(BF)

    stages = (third, third_res, fourth, fourth_res)
    chunks = ROWS // CHUNK
    for step in range(chunks + len(stages) - 1):
        for behind in reversed(range(len(stages))):
            n = step - behind
            if 0 <= n < chunks:
                lo = max(0, n * CHUNK - behind * CD)
                hi = ROWS if n == chunks - 1 else (n + 1) * CHUNK - behind * CD
                stages[behind](lo, hi)

    near = [
        jnp.concatenate([a4[(16 * half + i) * CD : (16 * half + i + 1) * CD, :] for half in range(2 * FR)], axis=0)
        for i in range(18)
    ]
    acc = dot(jnp.concatenate(near, axis=1), wc[...].reshape(18 * 256, 128))
    wave = (jnp.tanh(acc) * win[...]).astype(BF)
    halves = [
        jnp.concatenate([wave[(2 * fr + h) * CD : (2 * fr + h + 1) * CD] for fr in range(FR)], axis=0)
        for h in range(2)
    ]
    out[...] = dot(disp[...], jnp.concatenate(halves, axis=1)).astype(BF)


def cut(hid, own, to1, to2, to3, sems):
    section = lax.axis_index("section")
    copies = []
    for d, block in ((1, to1), (2, to2), (3, to3), (0, own)):
        rows = pl.ds(pl.multiple_of(lax.rem(section + d, SECT) * 128, 128), 128)
        copies.append(pltpu.make_async_copy(hid.at[rows, :], block, sems.at[d]))
        copies[-1].start()
    for copy in copies:
        copy.wait()


def place(plac, rec, out):
    y = dot(plac[...], rec[...])
    out[pl.ds(0, 256, stride=2), :] = y[:, 0:128]
    out[pl.ds(1, 256, stride=2), :] = y[:, 128:256]


VM = pl.BlockSpec(memory_space=pltpu.VMEM)
HB = pl.BlockSpec(memory_space=pltpu.HBM)
LIMIT = 33 * 1024 * 1024


def shards(
    hidden, pre_weight, up1_weight, up2_weight, up3_weight, res3_weight, up4_weight, res4_weight,
    post_weight, owner_device, stream_slot, start_frame, lead_frames, tail_frames,
):
    shape = jax.ShapeDtypeStruct
    own, *outgoing = pl.pallas_call(
        cut,
        out_shape=(shape((128, 256), BF),) * 4,
        in_specs=[HB],
        out_specs=(VM,) * 4,
        scratch_shapes=[pltpu.SemaphoreType.DMA((SECT,))],
        compiler_params=pltpu.CompilerParams(vmem_limit_bytes=4 * 1024 * 1024),
        name="cut",
    )(pltpu.with_memory_space_constraint(hidden.reshape(512, 256), pltpu.HBM))
    received = [
        lax.ppermute(block, "section", [(i, (i + d) % SECT) for i in range(SECT)])
        for d, block in zip((1, 2, 3), outgoing)
    ]
    prepared = pl.pallas_call(
        prepare,
        out_shape=(
            shape((16, 512, 256), BF),
            shape((8, 256, 256), BF),
            shape((512, 256), BF),
            shape((768, 256), BF),
            shape((512, 256), BF),
            shape((512, 256), BF),
            shape((18, 256, 128), BF),
            shape((512, 128), BF),
            shape((256, 512), BF),
            shape((256, 128), F32),
        ),
        in_specs=[HB] * 12,
        out_specs=(VM,) * 10,
        scratch_shapes=[
            pltpu.VMEM((7, 32), BF),
            pltpu.VMEM((4, 64, 128), BF),
            pltpu.VMEM((3, 64, 64), BF),
            pltpu.VMEM((4, 32, 64), BF),
            pltpu.VMEM((3, 32, 32), BF),
            pltpu.VMEM((1, 2048), jnp.int32),
            *[pltpu.VMEM((16, 128), jnp.int32)] * 4,
            pltpu.VMEM((16, 256, 128), BF),
            pltpu.VMEM((128, 128), F32),
            pltpu.SemaphoreType.DMA((12,)),
        ],
        compiler_params=pltpu.CompilerParams(vmem_limit_bytes=14 * 1024 * 1024),
        cost_estimate=pl.CostEstimate(flops=2_000_000_000, bytes_accessed=8_000_000, transcendentals=0),
        name="prepare",
    )(
        *(
            pltpu.with_memory_space_constraint(v, pltpu.HBM)
            for v in (
                post_weight, jnp.swapaxes(up3_weight, 1, 2), res3_weight, jnp.swapaxes(up4_weight, 1, 2),
                res4_weight, owner_device.reshape(1, 2048),
                *(v.reshape(16, 128) for v in (stream_slot, start_frame, lead_frames, tail_frames)),
                up2_weight,
                up1_weight,
            )
        )
    )
    up1, w2p, b3, r3, b4, r4, wc, disp, plac, win = prepared
    sent = pl.pallas_call(
        synthesize,
        out_shape=shape((512, 256), BF),
        in_specs=[VM] * 14,
        out_specs=VM,
        scratch_shapes=[
            pltpu.VMEM((128 + 6 * CD, 1024), BF),
            pltpu.VMEM((128 + 2 * CD, 512), BF),
            pltpu.VMEM((1024 + 2 * CD, 256), BF),
            pltpu.VMEM((ROWS + 2 * CD, 256), BF),
            pltpu.VMEM((ROWS, 256), F32),
            pltpu.VMEM((ROWS + 2 * CD, 256), BF),
            pltpu.VMEM((ROWS + 2 * CD, 256), BF),
            pltpu.VMEM((ROWS, 256), F32),
            pltpu.VMEM((ROWS + 2 * CD, 256), BF),
            pltpu.VMEM((ROWS + 2 * CD, 256), BF),
        ],
        compiler_params=pltpu.CompilerParams(vmem_limit_bytes=LIMIT),
        cost_estimate=pl.CostEstimate(
            flops=8_000_000_000, bytes_accessed=20_000_000, transcendentals=32768
        ),
        name="synthesize",
    )(own, *received, pre_weight, up1, w2p, b3, r3, b4, r4, wc, disp, win)
    waves = lax.all_to_all(sent, "group", split_axis=0, concat_axis=0, tiled=True)
    streams = pl.pallas_call(
        place,
        out_shape=shape((512, 128), F32),
        in_specs=[VM] * 2,
        out_specs=VM,
        compiler_params=pltpu.CompilerParams(vmem_limit_bytes=8 * 1024 * 1024),
        name="place",
    )(plac, waves)
    return streams.reshape(4, 1, 64 * HOP)


def solution(mesh):
    in_specs = (P("group", None, "section"),) + (P(),) * 13
    return jax.shard_map(
        shards, mesh=mesh, in_specs=in_specs, out_specs=P("group", "section", None), check_vma=False
    )
```

```python
import jax
import jax.numpy as jnp
from jax import lax
from jax.experimental import pallas as pl
from jax.experimental.pallas import tpu as pltpu
from jax.sharding import PartitionSpec as P

CD = 16
FR = 8
SECT = 4
LANES = 32
HOP = 256
SUPER = 256
ROWS = SUPER * CD
BF = jnp.bfloat16
F32 = jnp.float32


def dot(a, b):
    return jnp.dot(a, b, preferred_element_type=F32)


def leaky(v, slope):
    return jnp.maximum(v, slope * v)


def iota(shape, dim):
    return lax.broadcasted_iota(jnp.int32, shape, dim)


def as_bf(mask):
    return jnp.where(mask, 1.0, 0.0).astype(BF)


def spread(flat, width):
    place = as_bf(iota((width, 256), 1) % width == iota((width, 256), 0))
    return dot(flat, place)


def spread_t(ref, width):
    place = as_bf(iota((width, 256), 1) % width == iota((width, 256), 0))
    return jnp.concatenate(
        [
            lax.dot_general(ref[j], place, (((0,), (0,)), ((), ())), preferred_element_type=F32)
            for j in range(ref.shape[0])
        ],
        axis=0,
    )


def blocks(rep, rows, width, entries):
    block_of = iota((rows, 256), 1) // width
    out = []
    for entry in entries:
        acc = jnp.zeros((rows, 256), F32)
        for q, j in entry:
            acc = jnp.where(block_of == q, rep[j * rows : (j + 1) * rows], acc)
        out.append(acc)
    return jnp.concatenate(out, axis=0).astype(BF)


def up_entries(places, phases):
    return [[(q, q + 1 - 2 * a) for q in range(phases) if 0 <= q + 1 - 2 * a <= 3] for a in places]


def res_entries(places, phases):
    return [
        [(q, (a - q) // 3 + 1) for q in range(phases) if a - q in (-3, 0, 3)] for a in places
    ]


def turn():
    r, c = iota((128, 128), 0), iota((128, 128), 1)
    return as_bf(c == (r % CD) * FR + r // CD)


def taps_of(ref, first):
    taps = [ref[j * CD : j * CD + 128, first : first + 256] for j in range(7)]
    return jnp.concatenate(taps, axis=1)


def prepare(*refs):
    (own, pre), sources, (part, b3, r3, b4, r4, wc, disp, plac, win) = refs[:2], refs[2:12], refs[12:21]
    held, (scr, xb, sems) = refs[21:31], refs[31:]
    copies = [pltpu.make_async_copy(a, b, sems.at[i]) for i, (a, b) in enumerate(zip(sources, held))]
    for copy in copies:
        copy.start()
    post, up3, res3, up4, res4, owners, slot, start, lead, tail = held
    section = lax.axis_index("section")
    lane = lax.axis_index("group")
    zero = jnp.zeros((3 * CD, 256), BF)
    xb[0 : 3 * CD, :] = zero
    xb[3 * CD + 128 :, :] = zero
    xb[3 * CD : 3 * CD + 128, :] = dot(turn(), own[...]).astype(BF)
    rows = pl.ds(pl.multiple_of(section * 256, 256), 256)
    part[...] = dot(taps_of(xb, 0), pre[:, rows, :].reshape(7 * 256, 512))
    for copy in copies:
        copy.wait()
    b3[...] = blocks(spread_t(up3, 64), 128, 64, up_entries((0, 1, 2, -1), 4))
    r3[...] = blocks(
        spread(res3[...].reshape(192, 64), 64), 64, 64, res_entries((*range(4), *range(-4, 0), *range(4, 8)), 4)
    )
    b4[...] = blocks(
        spread_t(up4, 32), 64, 32, up_entries((*range(4), 4, 5, -2, -1), 8)
    )
    r4[...] = blocks(
        spread(res4[...].reshape(96, 32), 32), 32, 32, res_entries((*range(8), *range(8, 12), *range(-4, 0)), 8)
    )
    scr[...] = jnp.zeros_like(scr)
    scr[0:7, 0:32] = post[...].astype(F32)
    post_t = jnp.transpose(scr[...])[0:32].astype(BF)
    tap, off = iota((128, 128), 0), iota((128, 128), 1)
    base = jnp.concatenate(
        [dot(post_t, as_bf((tap == a + 6 - off) & (tap < 7))) for a in range(8)], axis=0
    ).astype(BF)
    off, smp = iota((128, 256), 0), iota((128, 256), 1)
    for i in range(9):
        first = jnp.where(smp < 128, 8 * (i - 1) - 3, 128 + 8 * (i + 8) - 3)
        both = dot(base, as_bf((smp == first + off) & (off < 14)))
        wc[i] = both[:, 0:128].astype(BF)
        wc[i + 9] = both[:, 128:256].astype(BF)
    owner = jnp.concatenate([owners[:, i * 128 : (i + 1) * 128] for i in range(16)], axis=0)
    mine = jnp.where(iota((16, 128), 0) == lane // 2, 1, 0)
    spot = lane % 2 * 64 + section * CD
    rowsel = lambda v: jnp.sum(v * mine, axis=0, keepdims=True).astype(F32)
    pick = iota((256, 128), 1) == spot + iota((256, 128), 0) % CD
    column = lambda v: jnp.sum(jnp.where(pick, rowsel(v), 0.0), axis=1, keepdims=True)
    owner_col = column(owner)[0:128]
    owner_row = jnp.sum(
        jnp.where(iota((128, 128), 0) == iota((128, 128), 1), owner_col, 0.0), axis=0, keepdims=True
    )
    before = (owner_col[0:CD] == owner_row) & (iota((CD, 128), 0) < iota((CD, 128), 1) % CD)
    rank = jnp.sum(jnp.where(before, 1.0, 0.0), axis=0, keepdims=True)
    dest = (2.0 * owner_row + rank).astype(jnp.int32)
    r_d, l_d = iota((512, 128), 0), iota((512, 128), 1)
    disp[...] = as_bf((r_d // FR == dest) & (r_d % FR == l_d // CD))
    t = ((iota((256, 128), 0) // CD) * 128 + iota((256, 128), 1)).astype(F32) + 0.5
    win[...] = jnp.minimum(1.0, t / (HOP * column(lead[...]))) * jnp.minimum(
        1.0, (FR * HOP - t) / (HOP * column(tail[...]))
    )
    l_g = iota((16, 128), 1)
    owned = jnp.where((l_g // CD % SECT == section) & (owner == lane), 1.0, 0.0)
    r_l, c_l = iota((128, 128), 0), iota((128, 128), 1)
    order = dot(owned.astype(BF), as_bf((r_l < c_l) & (r_l // 64 == c_l // 64)))
    target = (slot[...] * 64 + start[...]).astype(F32) * owned
    l_p = iota((16, 512), 1)
    item = jnp.zeros((16, 512), F32)
    for half in range(2):
        for c in range(2):
            at = jnp.sum(
                jnp.where((order == float(c)) & (l_g // 64 == half), target, 0.0), axis=1, keepdims=True
            )
            item = jnp.where(l_p // FR % 4 == 2 * half + c, at, item)
    item = jnp.where(l_p // 32 == iota((16, 512), 0), item, 0.0)
    goal = jnp.sum(item, axis=0, keepdims=True).astype(jnp.int32) + iota((1, 512), 1) % FR
    plac[...] = as_bf(iota((256, 512), 0) == goal)


def edges(ref, first, rows):
    return jnp.concatenate(
        [ref[first + 2 * CD : first + 2 * CD + rows, 0:128], ref[first : first + rows, 128:256]], axis=1
    )


CHUNK = 512


def synthesize(
    part, rec1, rec2, rec3, pre, up1, up2, b3, r3, b4, r4, wc, disp, win, out,
    xb, a0, a1, a2, u3, i3, a3, u4, i4, a4,
):
    section = lax.axis_index("section")
    for ref, pad in ((xb, 3), (a0, 1), (a1, 1), (a2, 1), (i3, 1), (a3, 1), (i4, 1), (a4, 1)):
        width = ref.shape[-1]
        zero = jnp.zeros((pad * CD, width), BF)
        ref[0 : pad * CD, :] = zero
        ref[ref.shape[0] - pad * CD :, :] = zero

    flip = turn()
    acc = part[...]
    for d, block in enumerate((rec1, rec2, rec3)):
        xb[3 * CD : 3 * CD + 128, d * 256 : (d + 1) * 256] = dot(flip, block[...]).astype(BF)
    for d in range(3):
        rows = pl.ds(pl.multiple_of(lax.rem(section + 3 - d, SECT) * 256, 256), 256)
        acc = acc + dot(taps_of(xb, d * 256), pre[:, rows, :].reshape(7 * 256, 512))
    a0[CD : CD + 128, :] = leaky(acc, 0.1).astype(BF)

    for p in range(8):
        shift, j = (0, p + 12) if p < 4 else (2 * CD, p - 4)
        y = dot(a0[CD : CD + 128, :], up1[p + 4]) + dot(a0[shift : shift + 128, :], up1[j])
        y = leaky(y, 0.1).astype(BF)
        for i in range(FR):
            at = (8 * i + p + 1) * CD
            a1[at : at + CD, :] = y[i * CD : (i + 1) * CD]

    for part in range(4):
        first = part * 256
        here = a1[first + CD : first + CD + 256, :]
        earlier = a1[first : first + 256, :]
        later = a1[first + 2 * CD : first + 2 * CD + 256, :]
        for q in range(4):
            side, j = (earlier, q + 6) if q < 2 else (later, q - 2)
            taps = [
                jnp.concatenate([up2[2 * k], up2[2 * k + 1]], axis=1) for k in (q + 2, j)
            ]
            pair = jnp.concatenate([here, side], axis=1)
            y = leaky(dot(pair, jnp.concatenate(taps, axis=0)), 0.1).astype(BF)
            for i in range(16):
                at = (4 * (part * 16 + i) + q + 1) * CD
                a2[at : at + CD, :] = y[i * CD : (i + 1) * CD]

    def third(lo, hi):
        rows = hi - lo
        y = dot(jnp.concatenate([a2[lo + CD : hi + CD, :], edges(a2, lo, rows)], axis=1), b3[...])
        u3[lo:hi, :] = y
        i3[lo + CD : hi + CD, :] = leaky(y, 0.1).astype(BF)

    def third_res(lo, hi):
        near = [i3[lo + CD : hi + CD, :], i3[lo:hi, :], i3[lo + 2 * CD : hi + 2 * CD, :]]
        y = u3[lo:hi, :] + dot(jnp.concatenate(near, axis=1), r3[...])
        a3[lo + CD : hi + CD, :] = leaky(y, 0.1).astype(BF)

    def fourth(lo, hi):
        rows = hi - lo
        y = dot(jnp.concatenate([a3[lo + CD : hi + CD, :], edges(a3, lo, rows)], axis=1), b4[...])
        u4[lo:hi, :] = y
        i4[lo + CD : hi + CD, :] = leaky(y, 0.1).astype(BF)

    def fourth_res(lo, hi):
        rows = hi - lo
        y = u4[lo:hi, :] + dot(
            jnp.concatenate([i4[lo + CD : hi + CD, :], edges(i4, lo, rows)], axis=1), r4[...]
        )
        a4[lo + CD : hi + CD, :] = leaky(y, 0.01).astype(BF)

    stages = (third, third_res, fourth, fourth_res)
    chunks = ROWS // CHUNK
    for step in range(chunks + len(stages) - 1):
        for behind in reversed(range(len(stages))):
            n = step - behind
            if 0 <= n < chunks:
                lo = max(0, n * CHUNK - behind * CD)
                hi = ROWS if n == chunks - 1 else (n + 1) * CHUNK - behind * CD
                stages[behind](lo, hi)

    near = [
        jnp.concatenate([a4[(16 * half + i) * CD : (16 * half + i + 1) * CD, :] for half in range(2 * FR)], axis=0)
        for i in range(18)
    ]
    acc = dot(jnp.concatenate(near, axis=1), wc[...].reshape(18 * 256, 128))
    wave = (jnp.tanh(acc) * win[...]).astype(BF)
    halves = [
        jnp.concatenate([wave[(2 * fr + h) * CD : (2 * fr + h + 1) * CD] for fr in range(FR)], axis=0)
        for h in range(2)
    ]
    out[...] = dot(disp[...], jnp.concatenate(halves, axis=1)).astype(BF)


def cut(hid, own, to1, to2, to3, sems):
    section = lax.axis_index("section")
    copies = []
    for d, block in ((1, to1), (2, to2), (3, to3), (0, own)):
        rows = pl.ds(pl.multiple_of(lax.rem(section + d, SECT) * 128, 128), 128)
        copies.append(pltpu.make_async_copy(hid.at[rows, :], block, sems.at[d]))
        copies[-1].start()
    for copy in copies:
        copy.wait()


def place(plac, rec, out):
    y = dot(plac[...], rec[...])
    out[pl.ds(0, 256, stride=2), :] = y[:, 0:128]
    out[pl.ds(1, 256, stride=2), :] = y[:, 128:256]


VM = pl.BlockSpec(memory_space=pltpu.VMEM)
HB = pl.BlockSpec(memory_space=pltpu.HBM)
LIMIT = 24 * 1024 * 1024


def shards(
    hidden, pre_weight, up1_weight, up2_weight, up3_weight, res3_weight, up4_weight, res4_weight,
    post_weight, owner_device, stream_slot, start_frame, lead_frames, tail_frames,
):
    shape = jax.ShapeDtypeStruct
    own, *outgoing = pl.pallas_call(
        cut,
        out_shape=(shape((128, 256), BF),) * 4,
        in_specs=[HB],
        out_specs=(VM,) * 4,
        scratch_shapes=[pltpu.SemaphoreType.DMA((SECT,))],
        compiler_params=pltpu.CompilerParams(vmem_limit_bytes=4 * 1024 * 1024),
        cost_estimate=pl.CostEstimate(flops=60_000_000_000, bytes_accessed=500_000, transcendentals=0),
        name="cut",
    )(pltpu.with_memory_space_constraint(hidden.reshape(512, 256), pltpu.HBM))
    received = [
        lax.ppermute(block, "section", [(i, (i + d) % SECT) for i in range(SECT)])
        for d, block in zip((1, 2, 3), outgoing)
    ]
    prepared = pl.pallas_call(
        prepare,
        out_shape=(
            shape((128, 512), F32),
            shape((512, 256), BF),
            shape((768, 256), BF),
            shape((512, 256), BF),
            shape((512, 256), BF),
            shape((18, 256, 128), BF),
            shape((512, 128), BF),
            shape((256, 512), BF),
            shape((256, 128), F32),
        ),
        in_specs=[VM] * 2 + [HB] * 10,
        out_specs=(VM,) * 9,
        scratch_shapes=[
            pltpu.VMEM((7, 32), BF),
            pltpu.VMEM((4, 64, 128), BF),
            pltpu.VMEM((3, 64, 64), BF),
            pltpu.VMEM((4, 32, 64), BF),
            pltpu.VMEM((3, 32, 32), BF),
            pltpu.VMEM((1, 2048), jnp.int32),
            *[pltpu.VMEM((16, 128), jnp.int32)] * 4,
            pltpu.VMEM((128, 128), F32),
            pltpu.VMEM((128 + 6 * CD, 256), BF),
            pltpu.SemaphoreType.DMA((10,)),
        ],
        compiler_params=pltpu.CompilerParams(vmem_limit_bytes=6 * 1024 * 1024),
        cost_estimate=pl.CostEstimate(flops=1000000000, bytes_accessed=4000000, transcendentals=0),
        name="prepare",
    )(
        own,
        pre_weight,
        *(
            pltpu.with_memory_space_constraint(v, pltpu.HBM)
            for v in (
                post_weight, jnp.swapaxes(up3_weight, 1, 2), res3_weight, jnp.swapaxes(up4_weight, 1, 2),
                res4_weight, owner_device.reshape(1, 2048),
                *(v.reshape(16, 128) for v in (stream_slot, start_frame, lead_frames, tail_frames)),
            )
        )
    )
    part, b3, r3, b4, r4, wc, disp, plac, win = prepared
    sent = pl.pallas_call(
        synthesize,
        out_shape=shape((512, 256), BF),
        in_specs=[VM] * 14,
        out_specs=VM,
        scratch_shapes=[
            pltpu.VMEM((128 + 6 * CD, 768), BF),
            pltpu.VMEM((128 + 2 * CD, 512), BF),
            pltpu.VMEM((1024 + 2 * CD, 256), BF),
            pltpu.VMEM((ROWS + 2 * CD, 256), BF),
            pltpu.VMEM((ROWS, 256), F32),
            pltpu.VMEM((ROWS + 2 * CD, 256), BF),
            pltpu.VMEM((ROWS + 2 * CD, 256), BF),
            pltpu.VMEM((ROWS, 256), F32),
            pltpu.VMEM((ROWS + 2 * CD, 256), BF),
            pltpu.VMEM((ROWS + 2 * CD, 256), BF),
        ],
        compiler_params=pltpu.CompilerParams(vmem_limit_bytes=LIMIT),
        cost_estimate=pl.CostEstimate(
            flops=8_000_000_000, bytes_accessed=20_000_000, transcendentals=32768
        ),
        name="synthesize",
    )(part, *received, pre_weight, up1_weight, up2_weight, b3, r3, b4, r4, wc, disp, win)
    waves = lax.all_to_all(sent, "group", split_axis=0, concat_axis=0, tiled=True)
    streams = pl.pallas_call(
        place,
        out_shape=shape((512, 128), F32),
        in_specs=[VM] * 2,
        out_specs=VM,
        compiler_params=pltpu.CompilerParams(vmem_limit_bytes=8 * 1024 * 1024),
        name="place",
    )(plac, waves)
    return streams.reshape(4, 1, 64 * HOP)


def solution(mesh):
    in_specs = (P("group", None, "section"),) + (P(),) * 13
    return jax.shard_map(
        shards, mesh=mesh, in_specs=in_specs, out_specs=P("group", "section", None), check_vma=False
    )
```

```python
import jax
import jax.numpy as jnp
from jax import lax
from jax.experimental import pallas as pl
from jax.experimental.pallas import tpu as pltpu
from jax.sharding import PartitionSpec as P

CD = 16
FR = 8
SECT = 4
LANES = 32
HOP = 256
SUPER = 256
ROWS = SUPER * CD
BF = jnp.bfloat16
F32 = jnp.float32


def dot(a, b):
    return jnp.dot(a, b, preferred_element_type=F32)


def leaky(v, slope):
    return jnp.maximum(v, slope * v)


def iota(shape, dim):
    return lax.broadcasted_iota(jnp.int32, shape, dim)


def as_bf(mask):
    return jnp.where(mask, 1.0, 0.0).astype(BF)


def spread(flat, width):
    place = as_bf(iota((width, 256), 1) % width == iota((width, 256), 0))
    return dot(flat, place)


def spread_t(ref, width):
    place = as_bf(iota((width, 256), 1) % width == iota((width, 256), 0))
    return jnp.concatenate(
        [
            lax.dot_general(ref[j], place, (((0,), (0,)), ((), ())), preferred_element_type=F32)
            for j in range(ref.shape[0])
        ],
        axis=0,
    )


def blocks(rep, rows, width, entries):
    block_of = iota((rows, 256), 1) // width
    out = []
    for entry in entries:
        acc = jnp.zeros((rows, 256), F32)
        for q, j in entry:
            acc = jnp.where(block_of == q, rep[j * rows : (j + 1) * rows], acc)
        out.append(acc)
    return jnp.concatenate(out, axis=0).astype(BF)


def up_entries(places, phases):
    return [[(q, q + 1 - 2 * a) for q in range(phases) if 0 <= q + 1 - 2 * a <= 3] for a in places]


def res_entries(places, phases):
    return [
        [(q, (a - q) // 3 + 1) for q in range(phases) if a - q in (-3, 0, 3)] for a in places
    ]


def turn():
    r, c = iota((128, 128), 0), iota((128, 128), 1)
    return as_bf(c == (r % CD) * FR + r // CD)


def taps_of(ref, first):
    taps = [ref[j * CD : j * CD + 128, first : first + 256] for j in range(7)]
    return jnp.concatenate(taps, axis=1)


def prepare(*refs):
    (own, pre), sources, (part, b3, r3, b4, r4, wc, disp, plac, win) = refs[:2], refs[2:12], refs[12:21]
    held, (scr, xb, sems) = refs[21:31], refs[31:]
    copies = [pltpu.make_async_copy(a, b, sems.at[i]) for i, (a, b) in enumerate(zip(sources, held))]
    for copy in copies:
        copy.start()
    post, up3, res3, up4, res4, owners, slot, start, lead, tail = held
    section = lax.axis_index("section")
    lane = lax.axis_index("group")
    zero = jnp.zeros((3 * CD, 256), BF)
    xb[0 : 3 * CD, :] = zero
    xb[3 * CD + 128 :, :] = zero
    xb[3 * CD : 3 * CD + 128, :] = dot(turn(), own[...]).astype(BF)
    rows = pl.ds(pl.multiple_of(section * 256, 256), 256)
    part[...] = dot(taps_of(xb, 0), pre[:, rows, :].reshape(7 * 256, 512))
    for copy in copies:
        copy.wait()
    b3[...] = blocks(spread_t(up3, 64), 128, 64, up_entries((0, 1, 2, -1), 4))
    r3[...] = blocks(
        spread(res3[...].reshape(192, 64), 64), 64, 64, res_entries((*range(4), *range(-4, 0), *range(4, 8)), 4)
    )
    b4[...] = blocks(
        spread_t(up4, 32), 64, 32, up_entries((*range(4), 4, 5, -2, -1), 8)
    )
    r4[...] = blocks(
        spread(res4[...].reshape(96, 32), 32), 32, 32, res_entries((*range(8), *range(8, 12), *range(-4, 0)), 8)
    )
    scr[...] = jnp.zeros_like(scr)
    scr[0:7, 0:32] = post[...].astype(F32)
    post_t = jnp.transpose(scr[...])[0:32].astype(BF)
    tap, off = iota((128, 128), 0), iota((128, 128), 1)
    base = jnp.concatenate(
        [dot(post_t, as_bf((tap == a + 6 - off) & (tap < 7))) for a in range(8)], axis=0
    ).astype(BF)
    off, smp = iota((128, 256), 0), iota((128, 256), 1)
    for i in range(9):
        first = jnp.where(smp < 128, 8 * (i - 1) - 3, 128 + 8 * (i + 8) - 3)
        both = dot(base, as_bf((smp == first + off) & (off < 14)))
        wc[i] = both[:, 0:128].astype(BF)
        wc[i + 9] = both[:, 128:256].astype(BF)
    owner = jnp.concatenate([owners[:, i * 128 : (i + 1) * 128] for i in range(16)], axis=0)
    mine = jnp.where(iota((16, 128), 0) == lane // 2, 1, 0)
    spot = lane % 2 * 64 + section * CD
    rowsel = lambda v: jnp.sum(v * mine, axis=0, keepdims=True).astype(F32)
    pick = iota((256, 128), 1) == spot + iota((256, 128), 0) % CD
    column = lambda v: jnp.sum(jnp.where(pick, rowsel(v), 0.0), axis=1, keepdims=True)
    owner_col = column(owner)[0:128]
    owner_row = jnp.sum(
        jnp.where(iota((128, 128), 0) == iota((128, 128), 1), owner_col, 0.0), axis=0, keepdims=True
    )
    before = (owner_col[0:CD] == owner_row) & (iota((CD, 128), 0) < iota((CD, 128), 1) % CD)
    rank = jnp.sum(jnp.where(before, 1.0, 0.0), axis=0, keepdims=True)
    dest = (2.0 * owner_row + rank).astype(jnp.int32)
    r_d, l_d = iota((512, 128), 0), iota((512, 128), 1)
    disp[...] = as_bf((r_d // FR == dest) & (r_d % FR == l_d // CD))
    t = ((iota((256, 128), 0) // CD) * 128 + iota((256, 128), 1)).astype(F32) + 0.5
    win[...] = jnp.minimum(1.0, t / (HOP * column(lead[...]))) * jnp.minimum(
        1.0, (FR * HOP - t) / (HOP * column(tail[...]))
    )
    l_g = iota((16, 128), 1)
    owned = jnp.where((l_g // CD % SECT == section) & (owner == lane), 1.0, 0.0)
    r_l, c_l = iota((128, 128), 0), iota((128, 128), 1)
    order = dot(owned.astype(BF), as_bf((r_l < c_l) & (r_l // 64 == c_l // 64)))
    target = (slot[...] * 64 + start[...]).astype(F32) * owned
    l_p = iota((16, 512), 1)
    item = jnp.zeros((16, 512), F32)
    for half in range(2):
        for c in range(2):
            at = jnp.sum(
                jnp.where((order == float(c)) & (l_g // 64 == half), target, 0.0), axis=1, keepdims=True
            )
            item = jnp.where(l_p // FR % 4 == 2 * half + c, at, item)
    item = jnp.where(l_p // 32 == iota((16, 512), 0), item, 0.0)
    goal = jnp.sum(item, axis=0, keepdims=True).astype(jnp.int32) + iota((1, 512), 1) % FR
    plac[...] = as_bf(iota((256, 512), 0) == goal)


def edges(ref, first, rows):
    return jnp.concatenate(
        [ref[first + 2 * CD : first + 2 * CD + rows, 0:128], ref[first : first + rows, 128:256]], axis=1
    )


CHUNK = 512


def synthesize(
    part, rec2, rec3, rec1, pre, up1, up2, b3, r3, b4, r4, wc, disp, win, out,
    xb, a0, a1, a2, u3, i3, a3, u4, i4, a4,
):
    section = lax.axis_index("section")
    for ref, pad in ((xb, 3), (a0, 1), (a1, 1), (a2, 1), (i3, 1), (a3, 1), (i4, 1), (a4, 1)):
        width = ref.shape[-1]
        zero = jnp.zeros((pad * CD, width), BF)
        ref[0 : pad * CD, :] = zero
        ref[ref.shape[0] - pad * CD :, :] = zero

    flip = turn()
    acc = part[...]
    for d, block in enumerate((rec1, rec2, rec3)):
        xb[3 * CD : 3 * CD + 128, d * 256 : (d + 1) * 256] = dot(flip, block[...]).astype(BF)
    for d in range(3):
        rows = pl.ds(pl.multiple_of((section ^ (d + 1)) * 256, 256), 256)
        acc = acc + dot(taps_of(xb, d * 256), pre[:, rows, :].reshape(7 * 256, 512))
    a0[CD : CD + 128, :] = leaky(acc, 0.1).astype(BF)

    for p in range(8):
        shift, j = (0, p + 12) if p < 4 else (2 * CD, p - 4)
        y = dot(a0[CD : CD + 128, :], up1[p + 4]) + dot(a0[shift : shift + 128, :], up1[j])
        y = leaky(y, 0.1).astype(BF)
        for i in range(FR):
            at = (8 * i + p + 1) * CD
            a1[at : at + CD, :] = y[i * CD : (i + 1) * CD]

    for part in range(4):
        first = part * 256
        here = a1[first + CD : first + CD + 256, :]
        earlier = a1[first : first + 256, :]
        later = a1[first + 2 * CD : first + 2 * CD + 256, :]
        for q in range(4):
            side, j = (earlier, q + 6) if q < 2 else (later, q - 2)
            taps = [
                jnp.concatenate([up2[2 * k], up2[2 * k + 1]], axis=1) for k in (q + 2, j)
            ]
            pair = jnp.concatenate([here, side], axis=1)
            y = leaky(dot(pair, jnp.concatenate(taps, axis=0)), 0.1).astype(BF)
            for i in range(16):
                at = (4 * (part * 16 + i) + q + 1) * CD
                a2[at : at + CD, :] = y[i * CD : (i + 1) * CD]

    def third(lo, hi):
        rows = hi - lo
        y = dot(jnp.concatenate([a2[lo + CD : hi + CD, :], edges(a2, lo, rows)], axis=1), b3[...])
        u3[lo:hi, :] = y
        i3[lo + CD : hi + CD, :] = leaky(y, 0.1).astype(BF)

    def third_res(lo, hi):
        near = [i3[lo + CD : hi + CD, :], i3[lo:hi, :], i3[lo + 2 * CD : hi + 2 * CD, :]]
        y = u3[lo:hi, :] + dot(jnp.concatenate(near, axis=1), r3[...])
        a3[lo + CD : hi + CD, :] = leaky(y, 0.1).astype(BF)

    def fourth(lo, hi):
        rows = hi - lo
        y = dot(jnp.concatenate([a3[lo + CD : hi + CD, :], edges(a3, lo, rows)], axis=1), b4[...])
        u4[lo:hi, :] = y
        i4[lo + CD : hi + CD, :] = leaky(y, 0.1).astype(BF)

    def fourth_res(lo, hi):
        rows = hi - lo
        y = u4[lo:hi, :] + dot(
            jnp.concatenate([i4[lo + CD : hi + CD, :], edges(i4, lo, rows)], axis=1), r4[...]
        )
        a4[lo + CD : hi + CD, :] = leaky(y, 0.01).astype(BF)

    stages = (third, third_res, fourth, fourth_res)
    chunks = ROWS // CHUNK
    for step in range(chunks + len(stages) - 1):
        for behind in reversed(range(len(stages))):
            n = step - behind
            if 0 <= n < chunks:
                lo = max(0, n * CHUNK - behind * CD)
                hi = ROWS if n == chunks - 1 else (n + 1) * CHUNK - behind * CD
                stages[behind](lo, hi)

    near = [
        jnp.concatenate([a4[(16 * half + i) * CD : (16 * half + i + 1) * CD, :] for half in range(2 * FR)], axis=0)
        for i in range(18)
    ]
    acc = dot(jnp.concatenate(near, axis=1), wc[...].reshape(18 * 256, 128))
    wave = (jnp.tanh(acc) * win[...]).astype(BF)
    halves = [
        jnp.concatenate([wave[(2 * fr + h) * CD : (2 * fr + h + 1) * CD] for fr in range(FR)], axis=0)
        for h in range(2)
    ]
    out[...] = dot(disp[...], jnp.concatenate(halves, axis=1)).astype(BF)


def cut(hid, own, to1, to2, to3, sems):
    section = lax.axis_index("section")
    copies = []
    for d, block in ((1, to1), (2, to2), (3, to3), (0, own)):
        rows = pl.ds(pl.multiple_of((section ^ d) * 128, 128), 128)
        copies.append(pltpu.make_async_copy(hid.at[rows, :], block, sems.at[d]))
        copies[-1].start()
    for copy in copies:
        copy.wait()


def place(plac, rec, out):
    y = dot(plac[...], rec[...])
    out[pl.ds(0, 256, stride=2), :] = y[:, 0:128]
    out[pl.ds(1, 256, stride=2), :] = y[:, 128:256]


VM = pl.BlockSpec(memory_space=pltpu.VMEM)
HB = pl.BlockSpec(memory_space=pltpu.HBM)
LIMIT = 24 * 1024 * 1024


def shards(
    hidden, pre_weight, up1_weight, up2_weight, up3_weight, res3_weight, up4_weight, res4_weight,
    post_weight, owner_device, stream_slot, start_frame, lead_frames, tail_frames,
):
    shape = jax.ShapeDtypeStruct
    own, *outgoing = pl.pallas_call(
        cut,
        out_shape=(shape((128, 256), BF),) * 4,
        in_specs=[HB],
        out_specs=(VM,) * 4,
        scratch_shapes=[pltpu.SemaphoreType.DMA((SECT,))],
        compiler_params=pltpu.CompilerParams(vmem_limit_bytes=4 * 1024 * 1024),
        cost_estimate=pl.CostEstimate(flops=60_000_000_000, bytes_accessed=500_000, transcendentals=0),
        name="cut",
    )(pltpu.with_memory_space_constraint(hidden.reshape(512, 256), pltpu.HBM))
    received = [
        lax.ppermute(block, "section", [(i, i ^ d) for i in range(SECT)])
        for d, block in zip((2, 3, 1), (outgoing[1], outgoing[2], outgoing[0]))
    ]
    prepared = pl.pallas_call(
        prepare,
        out_shape=(
            shape((128, 512), F32),
            shape((512, 256), BF),
            shape((768, 256), BF),
            shape((512, 256), BF),
            shape((512, 256), BF),
            shape((18, 256, 128), BF),
            shape((512, 128), BF),
            shape((256, 512), BF),
            shape((256, 128), F32),
        ),
        in_specs=[VM] * 2 + [HB] * 10,
        out_specs=(VM,) * 9,
        scratch_shapes=[
            pltpu.VMEM((7, 32), BF),
            pltpu.VMEM((4, 64, 128), BF),
            pltpu.VMEM((3, 64, 64), BF),
            pltpu.VMEM((4, 32, 64), BF),
            pltpu.VMEM((3, 32, 32), BF),
            pltpu.VMEM((1, 2048), jnp.int32),
            *[pltpu.VMEM((16, 128), jnp.int32)] * 4,
            pltpu.VMEM((128, 128), F32),
            pltpu.VMEM((128 + 6 * CD, 256), BF),
            pltpu.SemaphoreType.DMA((10,)),
        ],
        compiler_params=pltpu.CompilerParams(vmem_limit_bytes=6 * 1024 * 1024),
        cost_estimate=pl.CostEstimate(flops=1000000000, bytes_accessed=4000000, transcendentals=0),
        name="prepare",
    )(
        own,
        pre_weight,
        *(
            pltpu.with_memory_space_constraint(v, pltpu.HBM)
            for v in (
                post_weight, jnp.swapaxes(up3_weight, 1, 2), res3_weight, jnp.swapaxes(up4_weight, 1, 2),
                res4_weight, owner_device.reshape(1, 2048),
                *(v.reshape(16, 128) for v in (stream_slot, start_frame, lead_frames, tail_frames)),
            )
        )
    )
    part, b3, r3, b4, r4, wc, disp, plac, win = prepared
    sent = pl.pallas_call(
        synthesize,
        out_shape=shape((512, 256), BF),
        in_specs=[VM] * 14,
        out_specs=VM,
        scratch_shapes=[
            pltpu.VMEM((128 + 6 * CD, 768), BF),
            pltpu.VMEM((128 + 2 * CD, 512), BF),
            pltpu.VMEM((1024 + 2 * CD, 256), BF),
            pltpu.VMEM((ROWS + 2 * CD, 256), BF),
            pltpu.VMEM((ROWS, 256), F32),
            pltpu.VMEM((ROWS + 2 * CD, 256), BF),
            pltpu.VMEM((ROWS + 2 * CD, 256), BF),
            pltpu.VMEM((ROWS, 256), F32),
            pltpu.VMEM((ROWS + 2 * CD, 256), BF),
            pltpu.VMEM((ROWS + 2 * CD, 256), BF),
        ],
        compiler_params=pltpu.CompilerParams(vmem_limit_bytes=LIMIT),
        cost_estimate=pl.CostEstimate(
            flops=8_000_000_000, bytes_accessed=20_000_000, transcendentals=32768
        ),
        name="synthesize",
    )(part, *received, pre_weight, up1_weight, up2_weight, b3, r3, b4, r4, wc, disp, win)
    waves = lax.all_to_all(sent, "group", split_axis=0, concat_axis=0, tiled=True)
    streams = pl.pallas_call(
        place,
        out_shape=shape((512, 128), F32),
        in_specs=[VM] * 2,
        out_specs=VM,
        compiler_params=pltpu.CompilerParams(vmem_limit_bytes=8 * 1024 * 1024),
        name="place",
    )(plac, waves)
    return streams.reshape(4, 1, 64 * HOP)


def solution(mesh):
    in_specs = (P("group", None, "section"),) + (P(),) * 13
    return jax.shard_map(
        shards, mesh=mesh, in_specs=in_specs, out_specs=P("group", "section", None), check_vma=False
    )
```
